768 devices in a mesh: ctx: 24 (over z, core), dp: 32 (over y, x).
Axes of the slice: x: 4, y: 8, z: 12, core: 2. Of those that a mesh axis runs over, the one named last changes fastest.
Arguments:
- query_proj: bfloat16 [98304, 32, 128], P(('dp', 'ctx')), parts along dimension 0, may hold values from -60 to 60
- key_proj: bfloat16 [98304, 4, 128], P(('dp', 'ctx')), parts along dimension 0, may hold values from -40 to 40
- value_projection: bfloat16 [98304, 4, 128], P(('dp', 'ctx')), parts along dimension 0, may hold values from -6 to 6
- lengths: int32 [1536], P('dp'), parts along dimension 0, may hold values from 1 to 384, 3072 in all
Outputs:
- attended: bfloat16 [98304, 32, 128], P(('dp', 'ctx')), parts along dimension 0
- log_sum: float32 [32, 98304], P(None, ('dp', 'ctx')), parts along dimension 1
The draws below stay inside these ranges and needn't reach their ends.
There are 32 independent parts, one for each index of `dp`. The reference program is written for one: setup_inputs(seed, part) draws one part's arguments, and reference() takes and returns one part's arrays. A program takes and returns all parts, laid end to end along the dimension named above; each array names one. Nothing has to cross between parts.
Inputs may be any that keep to these rules, and one draw needn't show every extreme that they name: The lengths sum to 3072; the longest document has exactly 384 tokens.
All inputs are finite; a program needn't handle non-finite values.
Results may differ from the reference program's by a relative error of at most 0.0028.
Values may be sent and summed in bfloat16 or wider, within the bound.
No kernel may reach another device: no remote copies, remote signals or barrier semaphores. Data moves between devices by JAX's collectives and lax.ppermute only.
A program may use at most 32 MiB of HBM per device.

```python
import math
import jax
import jax.numpy as jnp
import numpy as np
from jax import lax

QUERY_HEADS = 32
KEY_VALUE_HEADS = 4
HEAD_SIZE = 128
SHARD_TOKENS = 128
PACKED_TOKENS = 3072
MAXDOC = 384
NDOC = 48


def shared_base(key):
    return jax.random.normal(key, (PACKED_TOKENS, KEY_VALUE_HEADS, HEAD_SIZE), jnp.float32)


def drawn_rows():
    row_numbers = jnp.arange(PACKED_TOKENS, dtype=jnp.int32)
    local_rows = row_numbers % SHARD_TOKENS
    shard_rows = row_numbers // SHARD_TOKENS
    even_shard = shard_rows % 2 == 0
    first_key = even_shard & (local_rows == SHARD_TOKENS - 12)
    second_key = even_shard & (local_rows == SHARD_TOKENS - 11)
    aligned_query = jnp.logical_not(even_shard) & (local_rows == 5)
    return (shard_rows, first_key, second_key, aligned_query)


def query_strength(shard_rows, start, step):
    return 3.0 * (start + step * (shard_rows // 2 % 4).astype(jnp.float32))


def draw_query_proj(key, part):
    base = shared_base(key)
    key = jax.random.fold_in(key, 5)
    shape = (PACKED_TOKENS, QUERY_HEADS, HEAD_SIZE)
    random_noise = jax.random.normal(key, shape, jnp.float32)
    start, step = (1.3, 0.5)
    shard_rows, first_key, second_key, aligned_query = drawn_rows()
    sink_direction = jnp.roll(base, 17, axis=0)
    aligned_rows = jnp.repeat(sink_direction, QUERY_HEADS // KEY_VALUE_HEADS, axis=1) * query_strength(shard_rows, start, step)[:, None, None]
    return jnp.where(aligned_query[:, None, None], aligned_rows, random_noise).astype(jnp.bfloat16)


def draw_key_proj(key, part):
    base = shared_base(key)
    key = jax.random.fold_in(key, 9)
    shape = (PACKED_TOKENS, KEY_VALUE_HEADS, HEAD_SIZE)
    random_noise = jax.random.normal(key, shape, jnp.float32)
    start, step = (1.3, 0.5)
    shard_rows, first_key, second_key, aligned_query = drawn_rows()
    shrink_by = 2.0 / (query_strength(shard_rows, start, step) * 6.0 * math.sqrt(HEAD_SIZE))
    first_rows = 6.0 * base
    second_rows = 6.0 * jnp.roll(base, 1, axis=0) * (1.0 - shrink_by)[:, None, None]
    planted = jnp.where(first_key[:, None, None], first_rows, jnp.where(second_key[:, None, None], second_rows, random_noise))
    return planted.astype(jnp.bfloat16)


def levels(key, dims, cuts, least, largest):
    loudness = 1.0
    for dim, shards_of in cuts:
        steps = jax.random.uniform(jax.random.fold_in(jax.random.fold_in(key, 6), dim), (shards_of,), jnp.float32, least / len(cuts), largest / len(cuts))
        loudness = loudness * jnp.repeat(jnp.exp(steps), dims[dim] // shards_of).reshape((-1,) + (1,) * (len(dims) - 1 - dim))
    return loudness


def profile(number_of, total, most, lean):
    weights = [(1 << 20) // math.isqrt(rank ** lean) + 1 for rank in range(2, number_of + 1)]
    surplus, counts = total - most - (number_of - 1), [1] * (number_of - 1)
    while surplus > 0:
        candidates = [i for i in range(number_of - 1) if counts[i] < most]
        pool, remaining = sum([weights[i] for i in candidates]), surplus
        for i in candidates:
            more = min(most - counts[i], max(1, remaining * weights[i] // pool), surplus)
            counts[i] = counts[i] + more
            surplus = surplus - more
    return np.array([most] + counts)


def uneven(own_key, number_of, total, most, lean):
    if number_of == 2:
        one = jax.random.randint(own_key, (), max(1, total - most), min(most, total - 1) + 1)
        return jnp.stack([one, total - one])
    sizes = jnp.asarray(profile(number_of, total, most, lean), jnp.int32)
    couples = (number_of - 1) // 2
    donor, sink = sizes[1:1 + 2 * couples:2], sizes[2:2 + 2 * couples:2]
    slack = jnp.minimum(donor - 1, most - sink)
    shifted = jax.random.randint(jax.random.fold_in(own_key, 1), (couples,), 0, 1 << 20) % (slack + 1)
    sizes = sizes.at[1:1 + 2 * couples:2].set(donor - shifted).at[2:2 + 2 * couples:2].set(sink + shifted)
    return sizes[jax.random.permutation(jax.random.fold_in(own_key, 2), number_of)]


def centred(key, dims, deviation, most, cuts=(), kind=jnp.bfloat16):
    loudness = levels(key, dims, cuts, -0.22, 0.18) if cuts else 1.0
    result = jax.random.normal(key, dims, jnp.float32) * deviation * loudness
    return jnp.minimum(jnp.maximum(result, -most), most).astype(kind)


def setup_inputs(seed: int = 0, part: int = 0) -> dict:
    key_of = jax.random.split(jax.random.key(seed), 5)
    part_keys = jax.random.split(jax.random.fold_in(key_of[4], part), 5)
    return {
        "query_proj": draw_query_proj(jax.random.fold_in(jax.random.fold_in(key_of[4], part), 71), part),
        "key_proj": draw_key_proj(jax.random.fold_in(jax.random.fold_in(key_of[4], part), 71), part),
        "value_projection": centred(part_keys[2], (PACKED_TOKENS, KEY_VALUE_HEADS, HEAD_SIZE), 1.0, 6.0, ((0, 24),)),
        "lengths": uneven(part_keys[3], NDOC, PACKED_TOKENS, MAXDOC, 2).astype(jnp.int32),
    }


def doc_index(positions, doc_ends):
    return lax.optimization_barrier(jnp.sum((doc_ends[None, :] <= positions[:, None]).astype(jnp.int32), axis=1))

def reference(query_proj, key_proj, value_projection, lengths):
    doc_ends = jnp.cumsum(lengths).astype(jnp.int32)
    positions = jnp.arange(PACKED_TOKENS, dtype=jnp.int32)
    key_docs = doc_index(positions, doc_ends)
    score_scale = 1.0 / math.sqrt(HEAD_SIZE)
    query_group_size = QUERY_HEADS // KEY_VALUE_HEADS
    key_float = key_proj.astype(jnp.float32)
    value_float = value_projection.astype(jnp.float32)

    def attend_block(offset):
        row_numbers = offset + jnp.arange(SHARD_TOKENS, dtype=jnp.int32)
        query_block = lax.dynamic_slice_in_dim(query_proj, offset, SHARD_TOKENS, 0).astype(jnp.float32)
        query_block = query_block.reshape(SHARD_TOKENS, KEY_VALUE_HEADS, query_group_size, HEAD_SIZE)
        scores = jnp.einsum('rhgd,khd->hgrk', query_block, key_float) * score_scale
        visible = (doc_index(row_numbers, doc_ends)[:, None] == key_docs[None, :]) & (positions[None, :] <= row_numbers[:, None])
        masked = jnp.where(visible, scores, -jnp.inf)
        row_max = lax.optimization_barrier(jnp.max(masked, axis=-1))
        probs = jnp.where(visible, jnp.exp(masked - row_max[..., None]), 0.0)
        row_sum = lax.optimization_barrier(jnp.sum(probs, axis=-1))
        weights = lax.optimization_barrier(probs.astype(jnp.bfloat16)).astype(jnp.float32)
        weighted = jnp.einsum('hgrk,khd->hgrd', weights, value_float)
        attended = (weighted / row_sum[..., None]).transpose(2, 0, 1, 3).reshape(SHARD_TOKENS, QUERY_HEADS, HEAD_SIZE).astype(jnp.bfloat16)
        log_sum = (row_max + jnp.log(row_sum)).reshape(QUERY_HEADS, SHARD_TOKENS)
        return (attended, log_sum)
    offsets = jnp.arange(PACKED_TOKENS // SHARD_TOKENS, dtype=jnp.int32) * SHARD_TOKENS
    attended_all, log_all = lax.map(attend_block, offsets)
    return (attended_all.reshape(PACKED_TOKENS, QUERY_HEADS, HEAD_SIZE), log_all.transpose(1, 0, 2).reshape(QUERY_HEADS, PACKED_TOKENS))
```

```python
import functools
import math

import jax
import jax.numpy as jnp
from jax import lax
from jax.experimental import pallas as pl
from jax.experimental.pallas import tpu as pltpu
from jax.sharding import PartitionSpec as P

hidden = -1e30
step_rows = 32


def lay_out_kernel(key_ref, value_ref, pair_ref, rows_ref):
    tokens, heads, _ = key_ref.shape
    for place, ref in enumerate((key_ref, value_ref)):
        rows_ref[...] = ref[...].astype(jnp.float32).reshape(rows_ref.shape)
        for head in range(heads):
            one = rows_ref[pl.ds(head, tokens, stride=heads), :]
            pair_ref[place * heads + head] = one.astype(jnp.bfloat16)


def lay_out(keys, values):
    tokens, heads, size = keys.shape
    return pl.pallas_call(
        lay_out_kernel,
        out_shape=jax.ShapeDtypeStruct((2 * heads, tokens, size), jnp.bfloat16),
        in_specs=[pl.BlockSpec(memory_space=pltpu.VMEM)] * 2,
        out_specs=pl.BlockSpec(memory_space=pltpu.VMEM),
        scratch_shapes=[pltpu.VMEM((tokens * heads, size), jnp.float32)],
        name="lay_out",
    )(keys, values)


def attend_kernel(
    lengths_ref,
    query_ref,
    own_ref,
    extra_ref,
    before_ref,
    out_ref,
    log_ref,
    key_ref,
    value_ref,
    bias_ref,
    top_ref,
    sum_ref,
):
    tokens, query_heads, size = query_ref.shape
    kv_heads = own_ref.shape[0] // 2
    group = query_heads // kv_heads
    scale = 1.0 / math.sqrt(size)
    shard = lax.axis_index("ctx")
    second = lax.rem(shard, 2) == 1
    base = shard * tokens

    lane = lax.broadcasted_iota(jnp.int32, (tokens, tokens), 1)
    row = lax.broadcasted_iota(jnp.int32, (tokens, tokens), 0)
    position = base + lane[:8]
    end = jnp.int32(0)
    start = jnp.int32(0)
    rows_of_first = jnp.int32(tokens)
    document = jnp.zeros((8, tokens), jnp.int32)
    for index in range(lengths_ref.shape[0]):
        end = end + lengths_ref[index]
        document = document + (end <= position).astype(jnp.int32)
        start = jnp.where(end <= base, end, start)
        inside = jnp.where(end > base, end - base, tokens)
        rows_of_first = jnp.minimum(rows_of_first, inside)
    reach = base - start
    remote_blocks = (reach + tokens - 1) // tokens

    by_key = jnp.broadcast_to(document[:1].astype(jnp.float32), (tokens, tokens))
    by_row = by_key.T
    own_bias = jnp.where((by_key == by_row) & (lane <= row), 0.0, hidden)
    bias_ref[3] = jnp.broadcast_to(own_bias[:, None, :], (tokens, group, tokens))
    for block in range(3):
        first_key = base - (3 - block) * tokens
        visible = (first_key + lane >= start) & (row < rows_of_first)
        bias = jnp.where(visible, 0.0, hidden)
        bias_ref[block] = jnp.broadcast_to(bias[:, None, :], (tokens, group, tokens))

    def place(block, pair, at):
        rows = slice(block * tokens, (block + 1) * tokens)
        for head in range(kv_heads):
            key_ref[head, rows, :] = pair[at + head]
            value_ref[head, rows, :size] = pair[at + kv_heads + head]

    for head in range(kv_heads):
        value_ref[head, :, size:] = jnp.ones((4 * tokens, size), jnp.bfloat16)
    place(3, own_ref, 0)

    @pl.when(second)
    def _():
        place(0, before_ref, 0)
        place(1, before_ref, 2 * kv_heads)
        place(2, extra_ref, 0)

    @pl.when(jnp.logical_not(second))
    def _():
        place(0, extra_ref, 0)
        place(1, before_ref, 0)
        place(2, before_ref, 2 * kv_heads)

    top_ref[...] = jnp.zeros_like(top_ref)
    sum_ref[...] = jnp.zeros_like(sum_ref)

    def attend_rows(first_row, blocks):
        low = 4 - blocks
        rows = pl.ds(first_row, step_rows)
        queries = query_ref[rows].astype(jnp.float32)
        hot = lax.broadcasted_iota(jnp.int32, (step_rows, group, tokens), 2) == (
            first_row + lax.broadcasted_iota(jnp.int32, (step_rows, group, tokens), 0)
        )
        results = []
        for head in range(kv_heads):
            lanes = slice(head * group, (head + 1) * group)
            one = queries[:, lanes, :].reshape(step_rows * group, size).astype(jnp.bfloat16)
            scores = lax.dot_general(
                one,
                key_ref[head, low * tokens :, :],
                (((1,), (1,)), ((), ())),
                preferred_element_type=jnp.float32,
            )
            parts = []
            for block in range(blocks):
                part = scores[:, block * tokens : (block + 1) * tokens]
                bias = bias_ref[low + block, rows]
                parts.append(part + bias.reshape(step_rows * group, tokens))
            most = functools.reduce(jnp.maximum, parts)
            top = jnp.max(most, axis=1, keepdims=True)
            weights = [jnp.exp((part - top) * scale).astype(jnp.bfloat16) for part in parts]
            total = jnp.dot(
                jnp.concatenate(weights, axis=1),
                value_ref[head, low * tokens :, :],
                preferred_element_type=jnp.float32,
            )
            row_sum = total[:, size:]
            result = total[:, :size] / row_sum
            results.append(result.reshape(step_rows, group, size))
            wide_top = jnp.broadcast_to(top, (step_rows * group, tokens))
            wide_top = wide_top.reshape(step_rows, group, tokens)
            wide_sum = row_sum.reshape(step_rows, group, tokens)
            top_ref[lanes, :] += jnp.sum(jnp.where(hot, wide_top, 0.0), axis=0)
            sum_ref[lanes, :] += jnp.sum(jnp.where(hot, wide_sum, 0.0), axis=0)
        out_ref[rows] = jnp.concatenate(results, axis=1).astype(jnp.bfloat16)

    @pl.loop(0, tokens // step_rows)
    def _(step):
        first_row = pl.multiple_of(step * step_rows, step_rows)
        needed = jnp.where(first_row < rows_of_first, remote_blocks, 0)
        for blocks in range(4):

            @pl.when(needed == blocks)
            def _():
                attend_rows(first_row, blocks + 1)

    log_ref[...] = top_ref[...] * scale + jnp.log(sum_ref[...])


def attend(lengths, queries, own, extra, before):
    tokens, query_heads, size = queries.shape
    kv_heads = own.shape[0] // 2
    group = query_heads // kv_heads
    vmem = pl.BlockSpec(memory_space=pltpu.VMEM)
    return pl.pallas_call(
        attend_kernel,
        out_shape=(
            jax.ShapeDtypeStruct((tokens, query_heads, size), jnp.bfloat16),
            jax.ShapeDtypeStruct((query_heads, tokens), jnp.float32),
        ),
        in_specs=[pl.BlockSpec(memory_space=pltpu.SMEM), vmem, vmem, vmem, vmem],
        out_specs=(vmem, vmem),
        scratch_shapes=[
            pltpu.VMEM((kv_heads, 4 * tokens, size), jnp.bfloat16),
            pltpu.VMEM((kv_heads, 4 * tokens, 2 * size), jnp.bfloat16),
            pltpu.VMEM((4, tokens, group, tokens), jnp.float32),
            pltpu.VMEM((query_heads, tokens), jnp.float32),
            pltpu.VMEM((query_heads, tokens), jnp.float32),
        ],
        compiler_params=pltpu.CompilerParams(vmem_limit_bytes=32 * 1024 * 1024),
        name="attend",
    )(lengths, queries, own, extra, before)


def per_device(query_proj, key_proj, value_projection, lengths):
    size = lax.axis_size("ctx")
    own = lay_out(key_proj, value_projection)
    by_two = [(i, i + 2) for i in range(size - 2)]
    pairs_of_chip = [[i, i + 1] for i in range(0, size, 2)]
    uneven = [(i, i + 1) for i in range(0, size, 2)] + [(i, i + 3) for i in range(1, size - 3, 2)]
    behind = lax.ppermute(own, "ctx", by_two)
    extra = lax.ppermute(own, "ctx", uneven)
    before = lax.all_gather(behind, "ctx", axis_index_groups=pairs_of_chip, axis=0, tiled=True)
    return attend(lengths, query_proj, own, extra, before)


def solution(mesh):
    return jax.shard_map(
        per_device,
        mesh=mesh,
        in_specs=(
            P(("dp", "ctx"), None, None),
            P(("dp", "ctx"), None, None),
            P(("dp", "ctx"), None, None),
            P("dp"),
        ),
        out_specs=(P(("dp", "ctx"), None, None), P(None, ("dp", "ctx"))),
        check_vma=False,
    )
```

```python
import functools
import math

import jax
import jax.numpy as jnp
from jax import lax
from jax.experimental import pallas as pl
from jax.experimental.pallas import tpu as pltpu
from jax.sharding import PartitionSpec as P

hidden = -1e30
half_rows = 64
chunk_rows = 16
pack_exponent = math.log2(math.e)


def prepare_kernel(
    all_lengths_ref, query_ref, grouped_ref, bias_ref, blocks_ref, lengths_ref, rows_ref, known, came
):
    tokens, query_heads, size = query_ref.shape
    kv_heads = grouped_ref.shape[0]
    group = query_heads // kv_heads
    part = tokens // 4
    lengths_copy = pltpu.make_async_copy(all_lengths_ref, lengths_ref, known)
    lengths_copy.start()
    copies = [
        pltpu.make_async_copy(
            query_ref.at[pl.ds(first, part)], rows_ref.at[pl.ds(first, part)], came.at[first // part]
        )
        for first in range(0, tokens, part)
    ]
    for copy in copies:
        copy.start()
    base = lax.axis_index("ctx") * tokens
    lane = lax.broadcasted_iota(jnp.int32, (tokens, tokens), 1)
    row = lax.broadcasted_iota(jnp.int32, (tokens, tokens), 0)
    position = base + lane[:8]
    end = jnp.int32(0)
    start = jnp.int32(0)
    rows_of_first = jnp.int32(tokens)
    document = jnp.zeros((8, tokens), jnp.int32)
    lengths_copy.wait()
    for index in range(lengths_ref.shape[0]):
        end = end + lengths_ref[index]
        document = document + (end <= position).astype(jnp.int32)
        start = jnp.where(end <= base, end, start)
        inside = jnp.where(end > base, end - base, tokens)
        rows_of_first = jnp.minimum(rows_of_first, inside)
    blocks_ref[...] = jnp.full(blocks_ref.shape, (base - start + tokens - 1) // tokens, jnp.int32)
    by_key = jnp.broadcast_to(document[:1].astype(jnp.float32), (tokens, tokens))
    by_row = by_key.T
    own_bias = jnp.where((by_key == by_row) & (lane <= row), 0.0, hidden)
    bias_ref[3] = jnp.broadcast_to(own_bias[:, None, :], (tokens, group, tokens))
    for block in range(3):
        first_key = base - (3 - block) * tokens
        visible = (first_key + lane >= start) & (row < rows_of_first)
        bias = jnp.where(visible, 0.0, hidden)
        bias_ref[block] = jnp.broadcast_to(bias[:, None, :], (tokens, group, tokens))
    for copy, first in zip(copies, range(0, tokens, part)):
        copy.wait()
        queries = rows_ref[first : first + part].astype(jnp.float32)
        for head in range(kv_heads):
            one = queries[:, head * group : (head + 1) * group, :].reshape(part * group, size)
            grouped_ref[head, first * group : (first + part) * group] = one.astype(jnp.bfloat16)


def prepare(lengths, queries, kv_heads):
    tokens, query_heads, size = queries.shape
    group = query_heads // kv_heads
    vmem = pl.BlockSpec(memory_space=pltpu.VMEM)
    return pl.pallas_call(
        prepare_kernel,
        out_shape=(
            jax.ShapeDtypeStruct((kv_heads, tokens * group, size), jnp.bfloat16),
            jax.ShapeDtypeStruct((4, tokens, group, tokens), jnp.float32),
            jax.ShapeDtypeStruct((8, 128), jnp.int32),
        ),
        in_specs=[pl.BlockSpec(memory_space=pltpu.HBM)] * 2,
        out_specs=(vmem, vmem, vmem),
        scratch_shapes=[
            pltpu.SMEM(lengths.shape, jnp.int32),
            pltpu.VMEM(queries.shape, jnp.bfloat16),
            pltpu.SemaphoreType.DMA,
            pltpu.SemaphoreType.DMA((4,)),
        ],
        compiler_params=pltpu.CompilerParams(vmem_limit_bytes=16 * 1024 * 1024),
        name="prepare",
    )(
        pltpu.with_memory_space_constraint(lengths, pltpu.HBM),
        pltpu.with_memory_space_constraint(queries, pltpu.HBM),
    )


def attend_kernel(
    blocks_ref,
    query_ref,
    bias_ref,
    own_ref,
    second_far_ref,
    first_near_ref,
    first_far_ref,
    second_near_ref,
    second_mid_ref,
    first_mid_ref,
    out_ref,
    log_ref,
    key_ref,
    value_ref,
    result_ref,
    rows_ref,
    logs_ref,
    totals_ref,
    sent,
    log_sent,
):
    kv_heads, stacked, size = query_ref.shape
    tokens = own_ref.shape[1]
    group = stacked // tokens
    scale = 1.0 / math.sqrt(size)
    shard = lax.axis_index("ctx")
    second = lax.rem(shard, 2) == 1
    remote_blocks = blocks_ref[0, 0]

    def place(block, pair_ref):
        rows = slice(block * tokens, (block + 1) * tokens)
        for head in range(kv_heads):
            key_ref[head, rows, :] = pair_ref[head]
            value_ref[head, rows, :size] = pair_ref[kv_heads + head]

    for head in range(kv_heads):
        value_ref[head, :, size:] = jnp.ones((4 * tokens, size), jnp.bfloat16)
    place(3, own_ref)

    @pl.when(second)
    def _():
        place(0, second_far_ref)
        place(1, second_mid_ref)
        place(2, second_near_ref)

    @pl.when(jnp.logical_not(second))
    def _():
        place(0, first_far_ref)
        place(1, first_mid_ref)
        place(2, first_near_ref)

    lane = lax.broadcasted_iota(jnp.int32, (group, tokens), 1)
    chunk = chunk_rows * group
    pairs, halves = kv_heads // 2, tokens // half_rows
    work = [
        (pair, 2 * pair + head, first)
        for pair in range(pairs)
        for head in range(2)
        for first in range(0, half_rows, chunk_rows)
    ]

    def copy_out(pair, half):
        rows = pl.ds(half * half_rows, half_rows)
        heads = pl.ds(2 * pair * group, 2 * group)
        return pltpu.make_async_copy(
            rows_ref.at[pair, half], out_ref.at[rows, heads], sent.at[pair, half]
        )

    def attend_half(half, blocks):
        low = 4 - blocks
        row_of_half = pl.multiple_of(half * half_rows, half_rows)
        logs = {
            head: tuple(
                totals_ref[part, head * group : (head + 1) * group, :] for part in range(2)
            )
            for head in range(kv_heads)
        }

        def score(item):
            _, head, first = item
            return lax.dot_general(
                query_ref[head, pl.ds((row_of_half + first) * group, chunk), :],
                key_ref[head, low * tokens :, :],
                (((1,), (1,)), ((), ())),
                preferred_element_type=jnp.float32,
            )

        def weigh(item, scores):
            _, _, first = item
            parts = []
            for block in range(blocks):
                part = scores[:, block * tokens : (block + 1) * tokens]
                bias = bias_ref[low + block, pl.ds(row_of_half + first, chunk_rows)]
                parts.append(part + bias.reshape(chunk, tokens))
            top = jnp.max(functools.reduce(jnp.maximum, parts), axis=1, keepdims=True)
            weights = [
                jnp.exp2((part - top) * (scale * pack_exponent)).astype(jnp.bfloat16)
                for part in parts
            ]
            return top, jnp.concatenate(weights, axis=1)

        def gather(item, top, weights):
            pair, head, first = item
            total = jnp.dot(
                weights, value_ref[head, low * tokens :, :], preferred_element_type=jnp.float32
            )
            row_sum = total[:, size:]
            share = pl.reciprocal(row_sum, approx=True)
            share = share * (2.0 - row_sum * share)
            result = total[:, :size] * share
            place_of_head = (head % 2) * group
            result_ref[
                pair, first : first + chunk_rows, place_of_head : place_of_head + group
            ] = result.reshape(chunk_rows, group, size)
            wide_top = jnp.broadcast_to(top, (chunk, tokens)).reshape(chunk_rows, group, tokens)
            wide_sum = row_sum.reshape(chunk_rows, group, tokens)
            tops, sums = logs[head]
            for row in range(chunk_rows):
                hot = lane == row_of_half + first + row
                tops = jnp.where(hot, wide_top[row], tops)
                sums = jnp.where(hot, wide_sum[row], sums)
            logs[head] = (tops, sums)
            if head % 2 == 1 and first + chunk_rows == half_rows:
                rows_ref[pair, half] = result_ref[pair].astype(jnp.bfloat16)
                copy_out(pair, half).start()

        scored, weighed = {}, {}
        count = len(work)
        for step in range(count + 2):
            if step < count:
                scored[step] = score(work[step])
            if 0 <= step - 1 < count:
                weighed[step - 1] = weigh(work[step - 1], scored.pop(step - 1))
            if 0 <= step - 2 < count:
                gather(work[step - 2], *weighed.pop(step - 2))
        for head in range(kv_heads):
            for part in range(2):
                totals_ref[part, head * group : (head + 1) * group, :] = logs[head][part]

    totals_ref[...] = jnp.ones_like(totals_ref)

    @pl.loop(0, halves)
    def _(half):
        @pl.when(remote_blocks < 2)
        def _():
            attend_half(half, 2)

        @pl.when(remote_blocks >= 2)
        def _():
            attend_half(half, 4)

    logs_ref[...] = totals_ref[0] * scale + jnp.log(totals_ref[1])
    log_copy = pltpu.make_async_copy(logs_ref, log_ref, log_sent)
    log_copy.start()
    for pair in range(pairs):
        for half in range(halves):
            copy_out(pair, half).wait()
    log_copy.wait()


def attend(prepared, own, earlier):
    grouped, bias, remote_blocks = prepared
    kv_heads, tokens, size = own.shape[0] // 2, own.shape[1], own.shape[2]
    group = grouped.shape[1] // tokens
    query_heads = kv_heads * group
    pairs, halves = kv_heads // 2, tokens // half_rows
    vmem = pl.BlockSpec(memory_space=pltpu.VMEM)
    return pl.pallas_call(
        attend_kernel,
        out_shape=(
            jax.ShapeDtypeStruct((tokens, query_heads, size), jnp.bfloat16),
            jax.ShapeDtypeStruct((query_heads, tokens), jnp.float32),
        ),
        in_specs=[vmem] * 10,
        out_specs=(pl.BlockSpec(memory_space=pl.ANY), pl.BlockSpec(memory_space=pl.ANY)),
        scratch_shapes=[
            pltpu.VMEM((kv_heads, 4 * tokens, size), jnp.bfloat16),
            pltpu.VMEM((kv_heads, 4 * tokens, 2 * size), jnp.bfloat16),
            pltpu.VMEM((pairs, half_rows, 2 * group, size), jnp.float32),
            pltpu.VMEM((pairs, halves, half_rows, 2 * group, size), jnp.bfloat16),
            pltpu.VMEM((query_heads, tokens), jnp.float32),
            pltpu.VMEM((2, query_heads, tokens), jnp.float32),
            pltpu.SemaphoreType.DMA((pairs, halves)),
            pltpu.SemaphoreType.DMA,
        ],
        compiler_params=pltpu.CompilerParams(vmem_limit_bytes=24 * 1024 * 1024),
        name="attend",
    )(remote_blocks, grouped, bias, own, *earlier)


def per_device(query_proj, key_proj, value_projection, lengths):
    size = lax.axis_size("ctx")
    tokens, kv_heads, head_size = key_proj.shape
    own = jnp.stack((key_proj, value_projection)).transpose(0, 2, 1, 3)
    own = own.reshape(2 * kv_heads, tokens, head_size)
    firsts, seconds = range(0, size, 2), range(1, size, 2)

    def move(array, starts, by):
        return lax.ppermute(array, "ctx", [(i, i + by) for i in starts if 0 <= i + by < size])

    second_mid = move(own, seconds, 2)
    first_mid = move(own, firsts, 2)
    second_near = move(own, firsts, 1)
    prepared = prepare(lengths, query_proj, kv_heads)
    passed_second, _ = lax.optimization_barrier((second_mid, prepared[2][:1, :1] * 3))
    passed_first, _ = lax.optimization_barrier((first_mid, prepared[2]))
    first_far = move(passed_second, seconds[1:], 1)
    first_near = move(passed_second, seconds[1:], -1)
    second_far = move(passed_first, firsts[1:], 1)
    earlier = (second_far, first_near, first_far, second_near, second_mid, first_mid)
    return attend(prepared, own, earlier)


def solution(mesh):
    return jax.shard_map(
        per_device,
        mesh=mesh,
        in_specs=(
            P(("dp", "ctx"), None, None),
            P(("dp", "ctx"), None, None),
            P(("dp", "ctx"), None, None),
            P("dp"),
        ),
        out_specs=(P(("dp", "ctx"), None, None), P(None, ("dp", "ctx"))),
        check_vma=False,
    )
```

```python
import functools
import math

import jax
import jax.numpy as jnp
from jax import lax
from jax.experimental import pallas as pl
from jax.experimental.pallas import tpu as pltpu
from jax.sharding import PartitionSpec as P

hidden = -1e30
half_rows = 64
chunk_rows = 16
pack_exponent = math.log2(math.e)


def prepare_kernel(
    all_lengths_ref, query_ref, grouped_ref, bias_ref, blocks_ref, lengths_ref, rows_ref, known, came
):
    tokens, query_heads, size = query_ref.shape
    kv_heads = grouped_ref.shape[0]
    group = query_heads // kv_heads
    part = tokens // 4
    lengths_copy = pltpu.make_async_copy(all_lengths_ref, lengths_ref, known)
    lengths_copy.start()
    copies = [
        pltpu.make_async_copy(
            query_ref.at[pl.ds(first, part)], rows_ref.at[pl.ds(first, part)], came.at[first // part]
        )
        for first in range(0, tokens, part)
    ]
    for copy in copies:
        copy.start()
    base = lax.axis_index("ctx") * tokens
    lane = lax.broadcasted_iota(jnp.int32, (tokens, tokens), 1)
    row = lax.broadcasted_iota(jnp.int32, (tokens, tokens), 0)
    position = base + lane[:8]
    end = jnp.int32(0)
    start = jnp.int32(0)
    rows_of_first = jnp.int32(tokens)
    document = jnp.zeros((8, tokens), jnp.int32)
    lengths_copy.wait()
    for index in range(lengths_ref.shape[0]):
        end = end + lengths_ref[index]
        document = document + (end <= position).astype(jnp.int32)
        start = jnp.where(end <= base, end, start)
        inside = jnp.where(end > base, end - base, tokens)
        rows_of_first = jnp.minimum(rows_of_first, inside)
    blocks_ref[...] = jnp.full(blocks_ref.shape, (base - start + tokens - 1) // tokens, jnp.int32)
    by_key = jnp.broadcast_to(document[:1].astype(jnp.float32), (tokens, tokens))
    by_row = by_key.T
    own_bias = jnp.where((by_key == by_row) & (lane <= row), 0.0, hidden)
    bias_ref[3] = jnp.broadcast_to(own_bias[:, None, :], (tokens, group, tokens))
    for block in range(3):
        first_key = base - (3 - block) * tokens
        visible = (first_key + lane >= start) & (row < rows_of_first)
        bias = jnp.where(visible, 0.0, hidden)
        bias_ref[block] = jnp.broadcast_to(bias[:, None, :], (tokens, group, tokens))
    for copy, first in zip(copies, range(0, tokens, part)):
        copy.wait()
        queries = rows_ref[first : first + part].astype(jnp.float32)
        for head in range(kv_heads):
            one = queries[:, head * group : (head + 1) * group, :].reshape(part * group, size)
            grouped_ref[head, first * group : (first + part) * group] = one.astype(jnp.bfloat16)


def prepare(lengths, queries, kv_heads):
    tokens, query_heads, size = queries.shape
    group = query_heads // kv_heads
    vmem = pl.BlockSpec(memory_space=pltpu.VMEM)
    return pl.pallas_call(
        prepare_kernel,
        out_shape=(
            jax.ShapeDtypeStruct((kv_heads, tokens * group, size), jnp.bfloat16),
            jax.ShapeDtypeStruct((4, tokens, group, tokens), jnp.float32),
            jax.ShapeDtypeStruct((8, 128), jnp.int32),
        ),
        in_specs=[pl.BlockSpec(memory_space=pltpu.HBM)] * 2,
        out_specs=(vmem, vmem, vmem),
        scratch_shapes=[
            pltpu.SMEM(lengths.shape, jnp.int32),
            pltpu.VMEM(queries.shape, jnp.bfloat16),
            pltpu.SemaphoreType.DMA,
            pltpu.SemaphoreType.DMA((4,)),
        ],
        compiler_params=pltpu.CompilerParams(vmem_limit_bytes=16 * 1024 * 1024),
        name="prepare",
    )(
        pltpu.with_memory_space_constraint(lengths, pltpu.HBM),
        pltpu.with_memory_space_constraint(queries, pltpu.HBM),
    )


def attend_kernel(
    blocks_ref,
    query_ref,
    bias_ref,
    own_ref,
    second_far_ref,
    first_near_ref,
    first_far_ref,
    second_near_ref,
    second_mid_ref,
    first_mid_ref,
    out_ref,
    log_ref,
    key_ref,
    value_ref,
    result_ref,
    rows_ref,
    logs_ref,
    totals_ref,
    sent,
    log_sent,
):
    kv_heads, stacked, size = query_ref.shape
    tokens = own_ref.shape[1]
    group = stacked // tokens
    scale = 1.0 / math.sqrt(size)
    shard = lax.axis_index("ctx")
    second = lax.rem(shard, 2) == 1
    remote_blocks = blocks_ref[0, 0]

    def place(block, pair_ref):
        rows = slice(block * tokens, (block + 1) * tokens)
        for head in range(kv_heads):
            key_ref[head, rows, :] = pair_ref[head]
            value_ref[head, rows, :size] = pair_ref[kv_heads + head]

    for head in range(kv_heads):
        value_ref[head, :, size:] = jnp.ones((4 * tokens, size), jnp.bfloat16)
    place(3, own_ref)

    @pl.when(second)
    def _():
        place(0, second_far_ref)
        place(1, second_mid_ref)
        place(2, second_near_ref)

    @pl.when(jnp.logical_not(second))
    def _():
        place(0, first_far_ref)
        place(1, first_mid_ref)
        place(2, first_near_ref)

    lane = lax.broadcasted_iota(jnp.int32, (group, tokens), 1)
    chunk = chunk_rows * group
    pairs, halves = kv_heads // 2, tokens // half_rows

    def copy_out(pair, half):
        rows = pl.ds(half * half_rows, half_rows)
        heads = pl.ds(2 * pair * group, 2 * group)
        return pltpu.make_async_copy(
            rows_ref.at[pair, half], out_ref.at[rows, heads], sent.at[pair, half]
        )

    def attend_rows(its_halves, blocks):
        low = 4 - blocks
        work = [
            (half, pair, 2 * pair + head, first)
            for half in its_halves
            for pair in range(pairs)
            for head in range(2)
            for first in range(0, half_rows, chunk_rows)
        ]

        def start_of(half, first):
            return half * half_rows + first

        logs = {
            head: tuple(
                totals_ref[part, head * group : (head + 1) * group, :] for part in range(2)
            )
            for head in range(kv_heads)
        }

        def score(item):
            half, _, head, first = item
            return lax.dot_general(
                query_ref[head, pl.ds(start_of(half, first) * group, chunk), :],
                key_ref[head, low * tokens :, :],
                (((1,), (1,)), ((), ())),
                preferred_element_type=jnp.float32,
            )

        def weigh(item, scores):
            half, _, _, first = item
            parts = []
            for block in range(blocks):
                part = scores[:, block * tokens : (block + 1) * tokens]
                bias = bias_ref[low + block, pl.ds(start_of(half, first), chunk_rows)]
                parts.append(part + bias.reshape(chunk, tokens))
            top = jnp.max(functools.reduce(jnp.maximum, parts), axis=1, keepdims=True)
            weights = [
                jnp.exp2((part - top) * (scale * pack_exponent)).astype(jnp.bfloat16)
                for part in parts
            ]
            return top, jnp.concatenate(weights, axis=1)

        def gather(item, top, weights):
            half, pair, head, first = item
            total = jnp.dot(
                weights, value_ref[head, low * tokens :, :], preferred_element_type=jnp.float32
            )
            row_sum = total[:, size:]
            share = pl.reciprocal(row_sum, approx=True)
            result = total[:, :size] * share
            place_of_head = (head % 2) * group
            result_ref[
                pair, first : first + chunk_rows, place_of_head : place_of_head + group
            ] = result.reshape(chunk_rows, group, size)
            wide_top = jnp.broadcast_to(top, (chunk, tokens)).reshape(chunk_rows, group, tokens)
            wide_sum = row_sum.reshape(chunk_rows, group, tokens)
            tops, sums = logs[head]
            for row in range(chunk_rows):
                hot = lane == start_of(half, first) + row
                tops = jnp.where(hot, wide_top[row], tops)
                sums = jnp.where(hot, wide_sum[row], sums)
            logs[head] = (tops, sums)
            if head % 2 == 1 and first + chunk_rows == half_rows:
                rows_ref[pair, half] = result_ref[pair].astype(jnp.bfloat16)
                copy_out(pair, half).start()

        scored, weighed = {}, {}
        count = len(work)
        for step in range(count + 2):
            if step < count:
                scored[step] = score(work[step])
            if 0 <= step - 1 < count:
                weighed[step - 1] = weigh(work[step - 1], scored.pop(step - 1))
            if 0 <= step - 2 < count:
                gather(work[step - 2], *weighed.pop(step - 2))
        for head in range(kv_heads):
            for part in range(2):
                totals_ref[part, head * group : (head + 1) * group, :] = logs[head][part]

    totals_ref[...] = jnp.ones_like(totals_ref)

    @pl.when(remote_blocks < 2)
    def _():
        @pl.loop(0, halves)
        def _(half):
            attend_rows([half], 2)

    @pl.when(remote_blocks >= 2)
    def _():
        attend_rows(range(halves), 4)

    logs_ref[...] = totals_ref[0] * scale + jnp.log(totals_ref[1])
    log_copy = pltpu.make_async_copy(logs_ref, log_ref, log_sent)
    log_copy.start()
    for pair in range(pairs):
        for half in range(halves):
            copy_out(pair, half).wait()
    log_copy.wait()


def attend(prepared, own, earlier):
    grouped, bias, remote_blocks = prepared
    kv_heads, tokens, size = own.shape[0] // 2, own.shape[1], own.shape[2]
    group = grouped.shape[1] // tokens
    query_heads = kv_heads * group
    pairs, halves = kv_heads // 2, tokens // half_rows
    vmem = pl.BlockSpec(memory_space=pltpu.VMEM)
    return pl.pallas_call(
        attend_kernel,
        out_shape=(
            jax.ShapeDtypeStruct((tokens, query_heads, size), jnp.bfloat16),
            jax.ShapeDtypeStruct((query_heads, tokens), jnp.float32),
        ),
        in_specs=[vmem] * 10,
        out_specs=(pl.BlockSpec(memory_space=pl.ANY), pl.BlockSpec(memory_space=pl.ANY)),
        scratch_shapes=[
            pltpu.VMEM((kv_heads, 4 * tokens, size), jnp.bfloat16),
            pltpu.VMEM((kv_heads, 4 * tokens, 2 * size), jnp.bfloat16),
            pltpu.VMEM((pairs, half_rows, 2 * group, size), jnp.float32),
            pltpu.VMEM((pairs, halves, half_rows, 2 * group, size), jnp.bfloat16),
            pltpu.VMEM((query_heads, tokens), jnp.float32),
            pltpu.VMEM((2, query_heads, tokens), jnp.float32),
            pltpu.SemaphoreType.DMA((pairs, halves)),
            pltpu.SemaphoreType.DMA,
        ],
        compiler_params=pltpu.CompilerParams(vmem_limit_bytes=24 * 1024 * 1024),
        name="attend",
    )(remote_blocks, grouped, bias, own, *earlier)


def per_device(query_proj, key_proj, value_projection, lengths):
    size = lax.axis_size("ctx")
    tokens, kv_heads, head_size = key_proj.shape
    own = jnp.stack((key_proj, value_projection)).transpose(0, 2, 1, 3)
    own = own.reshape(2 * kv_heads, tokens, head_size)
    firsts, seconds = range(0, size, 2), range(1, size, 2)

    def move(array, starts, by):
        return lax.ppermute(array, "ctx", [(i, i + by) for i in starts if 0 <= i + by < size])

    second_mid = move(own, seconds, 2)
    first_mid = move(own, firsts, 2)
    second_near = move(own, firsts, 1)
    prepared = prepare(lengths, query_proj, kv_heads)
    first_far = move(second_mid, seconds[1:], 1)
    first_near = move(second_mid, seconds[1:], -1)
    second_far = move(first_mid, firsts[1:], 1)
    earlier = (second_far, first_near, first_far, second_near, second_mid, first_mid)
    return attend(prepared, own, earlier)


def solution(mesh):
    return jax.shard_map(
        per_device,
        mesh=mesh,
        in_specs=(
            P(("dp", "ctx"), None, None),
            P(("dp", "ctx"), None, None),
            P(("dp", "ctx"), None, None),
            P("dp"),
        ),
        out_specs=(P(("dp", "ctx"), None, None), P(None, ("dp", "ctx"))),
        check_vma=False,
    )
```

```python
import functools
import math

import jax
import jax.numpy as jnp
from jax import lax
from jax.experimental import pallas as pl
from jax.experimental.pallas import tpu as pltpu
from jax.sharding import PartitionSpec as P

hidden = -1e30
half_rows = 64
chunk_rows = 16
pack_exponent = math.log2(math.e)


def prepare_kernel(
    all_lengths_ref, query_ref, grouped_ref, bias_ref, blocks_ref, lengths_ref, rows_ref, known, came
):
    tokens, query_heads, size = query_ref.shape
    kv_heads = grouped_ref.shape[0]
    group = query_heads // kv_heads
    part = tokens // 4
    lengths_copy = pltpu.make_async_copy(all_lengths_ref, lengths_ref, known)
    lengths_copy.start()
    copies = [
        pltpu.make_async_copy(
            query_ref.at[pl.ds(first, part)], rows_ref.at[pl.ds(first, part)], came.at[first // part]
        )
        for first in range(0, tokens, part)
    ]
    for copy in copies:
        copy.start()
    base = lax.axis_index("ctx") * tokens
    lane = lax.broadcasted_iota(jnp.int32, (tokens, tokens), 1)
    row = lax.broadcasted_iota(jnp.int32, (tokens, tokens), 0)
    position = base + lane[:8]
    end = jnp.int32(0)
    start = jnp.int32(0)
    rows_of_first = jnp.int32(tokens)
    document = jnp.zeros((8, tokens), jnp.int32)
    lengths_copy.wait()
    for index in range(lengths_ref.shape[0]):
        end = end + lengths_ref[index]
        document = document + (end <= position).astype(jnp.int32)
        start = jnp.where(end <= base, end, start)
        inside = jnp.where(end > base, end - base, tokens)
        rows_of_first = jnp.minimum(rows_of_first, inside)
    blocks_ref[...] = jnp.full(blocks_ref.shape, (base - start + tokens - 1) // tokens, jnp.int32)
    by_key = jnp.broadcast_to(document[:1].astype(jnp.float32), (tokens, tokens))
    by_row = by_key.T
    own_bias = jnp.where((by_key == by_row) & (lane <= row), 0.0, hidden)
    bias_ref[3] = jnp.broadcast_to(own_bias[:, None, :], (tokens, group, tokens))
    for block in range(3):
        first_key = base - (3 - block) * tokens
        visible = (first_key + lane >= start) & (row < rows_of_first)
        bias = jnp.where(visible, 0.0, hidden)
        bias_ref[block] = jnp.broadcast_to(bias[:, None, :], (tokens, group, tokens))
    for copy, first in zip(copies, range(0, tokens, part)):
        copy.wait()
        queries = rows_ref[first : first + part].astype(jnp.float32)
        for head in range(kv_heads):
            one = queries[:, head * group : (head + 1) * group, :].reshape(part * group, size)
            grouped_ref[head, first * group : (first + part) * group] = one.astype(jnp.bfloat16)


def prepare(lengths, queries, kv_heads):
    tokens, query_heads, size = queries.shape
    group = query_heads // kv_heads
    vmem = pl.BlockSpec(memory_space=pltpu.VMEM)
    return pl.pallas_call(
        prepare_kernel,
        out_shape=(
            jax.ShapeDtypeStruct((kv_heads, tokens * group, size), jnp.bfloat16),
            jax.ShapeDtypeStruct((4, tokens, group, tokens), jnp.float32),
            jax.ShapeDtypeStruct((8, 128), jnp.int32),
        ),
        in_specs=[pl.BlockSpec(memory_space=pltpu.HBM)] * 2,
        out_specs=(vmem, vmem, vmem),
        scratch_shapes=[
            pltpu.SMEM(lengths.shape, jnp.int32),
            pltpu.VMEM(queries.shape, jnp.bfloat16),
            pltpu.SemaphoreType.DMA,
            pltpu.SemaphoreType.DMA((4,)),
        ],
        compiler_params=pltpu.CompilerParams(vmem_limit_bytes=16 * 1024 * 1024),
        name="prepare",
    )(
        pltpu.with_memory_space_constraint(lengths, pltpu.HBM),
        pltpu.with_memory_space_constraint(queries, pltpu.HBM),
    )


def attend_kernel(
    blocks_ref,
    query_ref,
    bias_ref,
    own_ref,
    second_far_ref,
    first_near_ref,
    first_far_ref,
    second_near_ref,
    second_mid_ref,
    first_mid_ref,
    out_ref,
    log_ref,
    key_ref,
    value_ref,
    result_ref,
    rows_ref,
    logs_ref,
    totals_ref,
    sent,
    log_sent,
):
    kv_heads, stacked, size = query_ref.shape
    tokens = own_ref.shape[1]
    group = stacked // tokens
    scale = 1.0 / math.sqrt(size)
    shard = lax.axis_index("ctx")
    second = lax.rem(shard, 2) == 1
    remote_blocks = blocks_ref[0, 0]

    def place(block, pair_ref):
        rows = slice(block * tokens, (block + 1) * tokens)
        for head in range(kv_heads):
            key_ref[head, rows, :] = pair_ref[head]
            value_ref[head, rows, :size] = pair_ref[kv_heads + head]

    for head in range(kv_heads):
        value_ref[head, :, size:] = jnp.ones((4 * tokens, size), jnp.bfloat16)
    place(3, own_ref)

    @pl.when(second)
    def _():
        place(0, second_far_ref)
        place(1, second_mid_ref)
        place(2, second_near_ref)

    @pl.when(jnp.logical_not(second))
    def _():
        place(0, first_far_ref)
        place(1, first_mid_ref)
        place(2, first_near_ref)

    lane = lax.broadcasted_iota(jnp.int32, (group, tokens), 1)
    chunk = chunk_rows * group
    pairs, halves = kv_heads // 2, tokens // half_rows

    def copy_out(pair, half):
        rows = pl.ds(half * half_rows, half_rows)
        heads = pl.ds(2 * pair * group, 2 * group)
        return pltpu.make_async_copy(
            rows_ref.at[pair, half], out_ref.at[rows, heads], sent.at[pair, half]
        )

    def attend_rows(its_halves, blocks):
        low = 4 - blocks
        work = [
            (half, pair, 2 * pair + head, first)
            for half in its_halves
            for pair in range(pairs)
            for head in range(2)
            for first in range(0, half_rows, chunk_rows)
        ]

        def start_of(half, first):
            return half * half_rows + first

        logs = {
            head: tuple(
                totals_ref[part, head * group : (head + 1) * group, :] for part in range(2)
            )
            for head in range(kv_heads)
        }

        def score(item):
            half, _, head, first = item
            return lax.dot_general(
                query_ref[head, pl.ds(start_of(half, first) * group, chunk), :],
                key_ref[head, low * tokens :, :],
                (((1,), (1,)), ((), ())),
                preferred_element_type=jnp.float32,
            )

        def weigh(item, scores):
            half, _, _, first = item
            parts = []
            for block in range(blocks):
                part = scores[:, block * tokens : (block + 1) * tokens]
                bias = bias_ref[low + block, pl.ds(start_of(half, first), chunk_rows)]
                parts.append(part + bias.reshape(chunk, tokens))
            top = jnp.max(functools.reduce(jnp.maximum, parts), axis=1, keepdims=True)
            weights = [
                jnp.exp2((part - top) * (scale * pack_exponent)).astype(jnp.bfloat16)
                for part in parts
            ]
            return top, jnp.concatenate(weights, axis=1)

        def gather(item, top, weights):
            half, pair, head, first = item
            total = jnp.dot(
                weights, value_ref[head, low * tokens :, :], preferred_element_type=jnp.float32
            )
            row_sum = total[:, size:]
            share = pl.reciprocal(row_sum, approx=True)
            result = total[:, :size] * share
            place_of_head = (head % 2) * group
            result_ref[
                pair, first : first + chunk_rows, place_of_head : place_of_head + group
            ] = result.reshape(chunk_rows, group, size)
            wide_top = jnp.broadcast_to(top, (chunk, tokens)).reshape(chunk_rows, group, tokens)
            wide_sum = row_sum.reshape(chunk_rows, group, tokens)
            tops, sums = logs[head]
            for row in range(chunk_rows):
                hot = lane == start_of(half, first) + row
                tops = jnp.where(hot, wide_top[row], tops)
                sums = jnp.where(hot, wide_sum[row], sums)
            logs[head] = (tops, sums)
            if head % 2 == 1 and first + chunk_rows == half_rows:
                rows_ref[pair, half] = result_ref[pair].astype(jnp.bfloat16)
                copy_out(pair, half).start()

        scored, weighed = {}, {}
        count = len(work)
        for step in range(count + 2):
            if step < count:
                scored[step] = score(work[step])
            if 0 <= step - 1 < count:
                weighed[step - 1] = weigh(work[step - 1], scored.pop(step - 1))
            if 0 <= step - 2 < count:
                gather(work[step - 2], *weighed.pop(step - 2))
        for head in range(kv_heads):
            for part in range(2):
                totals_ref[part, head * group : (head + 1) * group, :] = logs[head][part]

    totals_ref[...] = jnp.ones_like(totals_ref)

    @pl.when(remote_blocks < 2)
    def _():
        @pl.loop(0, halves)
        def _(half):
            attend_rows([half], 2)

    @pl.when(remote_blocks == 2)
    def _():
        attend_rows(range(halves), 3)

    @pl.when(remote_blocks > 2)
    def _():
        attend_rows(range(halves), 4)

    logs_ref[...] = totals_ref[0] * scale + jnp.log(totals_ref[1])
    log_copy = pltpu.make_async_copy(logs_ref, log_ref, log_sent)
    log_copy.start()
    for pair in range(pairs):
        for half in range(halves):
            copy_out(pair, half).wait()
    log_copy.wait()


def attend(prepared, own, earlier):
    grouped, bias, remote_blocks = prepared
    kv_heads, tokens, size = own.shape[0] // 2, own.shape[1], own.shape[2]
    group = grouped.shape[1] // tokens
    query_heads = kv_heads * group
    pairs, halves = kv_heads // 2, tokens // half_rows
    vmem = pl.BlockSpec(memory_space=pltpu.VMEM)
    return pl.pallas_call(
        attend_kernel,
        out_shape=(
            jax.ShapeDtypeStruct((tokens, query_heads, size), jnp.bfloat16),
            jax.ShapeDtypeStruct((query_heads, tokens), jnp.float32),
        ),
        in_specs=[vmem] * 10,
        out_specs=(pl.BlockSpec(memory_space=pl.ANY), pl.BlockSpec(memory_space=pl.ANY)),
        scratch_shapes=[
            pltpu.VMEM((kv_heads, 4 * tokens, size), jnp.bfloat16),
            pltpu.VMEM((kv_heads, 4 * tokens, 2 * size), jnp.bfloat16),
            pltpu.VMEM((pairs, half_rows, 2 * group, size), jnp.float32),
            pltpu.VMEM((pairs, halves, half_rows, 2 * group, size), jnp.bfloat16),
            pltpu.VMEM((query_heads, tokens), jnp.float32),
            pltpu.VMEM((2, query_heads, tokens), jnp.float32),
            pltpu.SemaphoreType.DMA((pairs, halves)),
            pltpu.SemaphoreType.DMA,
        ],
        compiler_params=pltpu.CompilerParams(vmem_limit_bytes=24 * 1024 * 1024),
        name="attend",
    )(remote_blocks, grouped, bias, own, *earlier)


def per_device(query_proj, key_proj, value_projection, lengths):
    size = lax.axis_size("ctx")
    tokens, kv_heads, head_size = key_proj.shape
    own = jnp.stack((key_proj, value_projection)).transpose(0, 2, 1, 3)
    own = own.reshape(2 * kv_heads, tokens, head_size)
    firsts, seconds = range(0, size, 2), range(1, size, 2)

    def move(array, starts, by):
        return lax.ppermute(array, "ctx", [(i, i + by) for i in starts if 0 <= i + by < size])

    second_mid = move(own, seconds, 2)
    first_mid = move(own, firsts, 2)
    second_near = move(own, firsts, 1)
    prepared = prepare(lengths, query_proj, kv_heads)
    first_far = move(second_mid, seconds[1:], 1)
    first_near = move(second_mid, seconds[1:], -1)
    second_far = move(first_mid, firsts[1:], 1)
    earlier = (second_far, first_near, first_far, second_near, second_mid, first_mid)
    return attend(prepared, own, earlier)


def solution(mesh):
    return jax.shard_map(
        per_device,
        mesh=mesh,
        in_specs=(
            P(("dp", "ctx"), None, None),
            P(("dp", "ctx"), None, None),
            P(("dp", "ctx"), None, None),
            P("dp"),
        ),
        out_specs=(P(("dp", "ctx"), None, None), P(None, ("dp", "ctx"))),
        check_vma=False,
    )
```

```python
import functools
import math

import jax
import jax.numpy as jnp
from jax import lax
from jax.experimental import pallas as pl
from jax.experimental.pallas import tpu as pltpu
from jax.sharding import PartitionSpec as P

hidden = -1e30
half_rows = 64
chunk_rows = 16
pack_exponent = math.log2(math.e)


def prepare_kernel(
    all_lengths_ref, query_ref, grouped_ref, bias_ref, reach_ref, lengths_ref, rows_ref, known, came
):
    tokens, query_heads, size = query_ref.shape
    kv_heads = grouped_ref.shape[0]
    group = query_heads // kv_heads
    part = tokens // 4
    lengths_copy = pltpu.make_async_copy(all_lengths_ref, lengths_ref, known)
    lengths_copy.start()
    copies = [
        pltpu.make_async_copy(
            query_ref.at[pl.ds(first, part)], rows_ref.at[pl.ds(first, part)], came.at[first // part]
        )
        for first in range(0, tokens, part)
    ]
    for copy in copies:
        copy.start()
    base = lax.axis_index("ctx") * tokens
    lane = lax.broadcasted_iota(jnp.int32, (tokens, tokens), 1)
    row = lax.broadcasted_iota(jnp.int32, (tokens, tokens), 0)
    position = base + lane[:8]
    end = jnp.int32(0)
    start = jnp.int32(0)
    rows_of_first = jnp.int32(tokens)
    document = jnp.zeros((8, tokens), jnp.int32)
    lengths_copy.wait()
    for index in range(lengths_ref.shape[0]):
        end = end + lengths_ref[index]
        document = document + (end <= position).astype(jnp.int32)
        start = jnp.where(end <= base, end, start)
        inside = jnp.where(end > base, end - base, tokens)
        rows_of_first = jnp.minimum(rows_of_first, inside)
    both = jnp.where(rows_of_first > half_rows, 1, 2)
    reach = jnp.where(base - start > tokens, both, 0)
    reach_ref[...] = jnp.full(reach_ref.shape, reach, jnp.int32)
    by_key = jnp.broadcast_to(document[:1].astype(jnp.float32), (tokens, tokens))
    by_row = by_key.T
    own_bias = jnp.where((by_key == by_row) & (lane <= row), 0.0, hidden)
    bias_ref[3] = jnp.broadcast_to(own_bias[:, None, :], (tokens, group, tokens))
    for block in range(3):
        first_key = base - (3 - block) * tokens
        visible = (first_key + lane >= start) & (row < rows_of_first)
        bias = jnp.where(visible, 0.0, hidden)
        bias_ref[block] = jnp.broadcast_to(bias[:, None, :], (tokens, group, tokens))
    for copy, first in zip(copies, range(0, tokens, part)):
        copy.wait()
        queries = rows_ref[first : first + part].astype(jnp.float32)
        for head in range(kv_heads):
            one = queries[:, head * group : (head + 1) * group, :].reshape(part * group, size)
            grouped_ref[head, first * group : (first + part) * group] = one.astype(jnp.bfloat16)


def prepare(lengths, queries, kv_heads):
    tokens, query_heads, size = queries.shape
    group = query_heads // kv_heads
    vmem = pl.BlockSpec(memory_space=pltpu.VMEM)
    return pl.pallas_call(
        prepare_kernel,
        out_shape=(
            jax.ShapeDtypeStruct((kv_heads, tokens * group, size), jnp.bfloat16),
            jax.ShapeDtypeStruct((4, tokens, group, tokens), jnp.float32),
            jax.ShapeDtypeStruct((8, 128), jnp.int32),
        ),
        in_specs=[pl.BlockSpec(memory_space=pltpu.HBM)] * 2,
        out_specs=(vmem, vmem, vmem),
        scratch_shapes=[
            pltpu.SMEM(lengths.shape, jnp.int32),
            pltpu.VMEM(queries.shape, jnp.bfloat16),
            pltpu.SemaphoreType.DMA,
            pltpu.SemaphoreType.DMA((4,)),
        ],
        compiler_params=pltpu.CompilerParams(vmem_limit_bytes=16 * 1024 * 1024),
        name="prepare",
    )(
        pltpu.with_memory_space_constraint(lengths, pltpu.HBM),
        pltpu.with_memory_space_constraint(queries, pltpu.HBM),
    )


def attend_kernel(
    reach_ref,
    query_ref,
    bias_ref,
    own_ref,
    second_far_ref,
    first_near_ref,
    first_far_ref,
    second_near_ref,
    second_mid_ref,
    first_mid_ref,
    out_ref,
    log_ref,
    key_ref,
    value_ref,
    result_ref,
    rows_ref,
    logs_ref,
    totals_ref,
    sent,
    log_sent,
):
    kv_heads, stacked, size = query_ref.shape
    tokens = own_ref.shape[1]
    group = stacked // tokens
    scale = 1.0 / math.sqrt(size)
    shard = lax.axis_index("ctx")
    second = lax.rem(shard, 2) == 1
    reach = reach_ref[0, 0]

    def place(block, pair_ref):
        rows = slice(block * tokens, (block + 1) * tokens)
        for head in range(kv_heads):
            key_ref[head, rows, :] = pair_ref[head]
            value_ref[head, rows, :size] = pair_ref[kv_heads + head]

    for head in range(kv_heads):
        value_ref[head, :, size:] = jnp.ones((4 * tokens, size), jnp.bfloat16)
    place(3, own_ref)

    @pl.when(second)
    def _():
        place(0, second_far_ref)
        place(1, second_mid_ref)
        place(2, second_near_ref)

    @pl.when(jnp.logical_not(second))
    def _():
        place(0, first_far_ref)
        place(1, first_mid_ref)
        place(2, first_near_ref)

    lane = lax.broadcasted_iota(jnp.int32, (group, tokens), 1)
    chunk = chunk_rows * group
    pairs, halves = kv_heads // 2, tokens // half_rows

    def copy_out(pair, half):
        rows = pl.ds(half * half_rows, half_rows)
        heads = pl.ds(2 * pair * group, 2 * group)
        return pltpu.make_async_copy(
            rows_ref.at[pair, half], out_ref.at[rows, heads], sent.at[pair, half]
        )

    def attend_rows(blocks_of):
        work = [
            (half, pair, 2 * pair + head, first)
            for half in range(halves)
            for pair in range(pairs)
            for head in range(2)
            for first in range(0, half_rows, chunk_rows)
        ]

        def start_of(half, first):
            return half * half_rows + first

        logs = {
            head: tuple(
                totals_ref[part, head * group : (head + 1) * group, :] for part in range(2)
            )
            for head in range(kv_heads)
        }

        def score(item):
            half, _, head, first = item
            low = 4 - blocks_of[half]
            return lax.dot_general(
                query_ref[head, pl.ds(start_of(half, first) * group, chunk), :],
                key_ref[head, low * tokens :, :],
                (((1,), (1,)), ((), ())),
                preferred_element_type=jnp.float32,
            )

        def weigh(item, scores):
            half, _, _, first = item
            blocks = blocks_of[half]
            low = 4 - blocks
            parts = []
            for block in range(blocks):
                part = scores[:, block * tokens : (block + 1) * tokens]
                bias = bias_ref[low + block, pl.ds(start_of(half, first), chunk_rows)]
                parts.append(part + bias.reshape(chunk, tokens))
            top = jnp.max(functools.reduce(jnp.maximum, parts), axis=1, keepdims=True)
            weights = [
                jnp.exp2((part - top) * (scale * pack_exponent)).astype(jnp.bfloat16)
                for part in parts
            ]
            return top, jnp.concatenate(weights, axis=1)

        def gather(item, top, weights):
            half, pair, head, first = item
            low = 4 - blocks_of[half]
            total = jnp.dot(
                weights, value_ref[head, low * tokens :, :], preferred_element_type=jnp.float32
            )
            row_sum = total[:, size:]
            share = pl.reciprocal(row_sum, approx=True)
            result = total[:, :size] * share
            place_of_head = (head % 2) * group
            result_ref[
                pair, first : first + chunk_rows, place_of_head : place_of_head + group
            ] = result.reshape(chunk_rows, group, size)
            wide_top = jnp.broadcast_to(top, (chunk, tokens)).reshape(chunk_rows, group, tokens)
            wide_sum = row_sum.reshape(chunk_rows, group, tokens)
            tops, sums = logs[head]
            for row in range(chunk_rows):
                hot = lane == start_of(half, first) + row
                tops = jnp.where(hot, wide_top[row], tops)
                sums = jnp.where(hot, wide_sum[row], sums)
            logs[head] = (tops, sums)
            if head % 2 == 1 and first + chunk_rows == half_rows:
                rows_ref[pair, half] = result_ref[pair].astype(jnp.bfloat16)
                copy_out(pair, half).start()

        scored, weighed = {}, {}
        count = len(work)
        for step in range(count + 2):
            if step < count:
                scored[step] = score(work[step])
            if 0 <= step - 1 < count:
                weighed[step - 1] = weigh(work[step - 1], scored.pop(step - 1))
            if 0 <= step - 2 < count:
                gather(work[step - 2], *weighed.pop(step - 2))
        for head in range(kv_heads):
            for part in range(2):
                totals_ref[part, head * group : (head + 1) * group, :] = logs[head][part]

    totals_ref[...] = jnp.ones_like(totals_ref)

    @pl.when(reach == 0)
    def _():
        attend_rows((2, 2))

    @pl.when(reach == 1)
    def _():
        attend_rows((4, 4))

    @pl.when(reach == 2)
    def _():
        attend_rows((4, 2))

    logs_ref[...] = totals_ref[0] * scale + jnp.log(totals_ref[1])
    log_copy = pltpu.make_async_copy(logs_ref, log_ref, log_sent)
    log_copy.start()
    for pair in range(pairs):
        for half in range(halves):
            copy_out(pair, half).wait()
    log_copy.wait()


def attend(prepared, own, earlier):
    grouped, bias, reach = prepared
    kv_heads, tokens, size = own.shape[0] // 2, own.shape[1], own.shape[2]
    group = grouped.shape[1] // tokens
    query_heads = kv_heads * group
    pairs, halves = kv_heads // 2, tokens // half_rows
    vmem = pl.BlockSpec(memory_space=pltpu.VMEM)
    return pl.pallas_call(
        attend_kernel,
        out_shape=(
            jax.ShapeDtypeStruct((tokens, query_heads, size), jnp.bfloat16),
            jax.ShapeDtypeStruct((query_heads, tokens), jnp.float32),
        ),
        in_specs=[vmem] * 10,
        out_specs=(pl.BlockSpec(memory_space=pl.ANY), pl.BlockSpec(memory_space=pl.ANY)),
        scratch_shapes=[
            pltpu.VMEM((kv_heads, 4 * tokens, size), jnp.bfloat16),
            pltpu.VMEM((kv_heads, 4 * tokens, 2 * size), jnp.bfloat16),
            pltpu.VMEM((pairs, half_rows, 2 * group, size), jnp.float32),
            pltpu.VMEM((pairs, halves, half_rows, 2 * group, size), jnp.bfloat16),
            pltpu.VMEM((query_heads, tokens), jnp.float32),
            pltpu.VMEM((2, query_heads, tokens), jnp.float32),
            pltpu.SemaphoreType.DMA((pairs, halves)),
            pltpu.SemaphoreType.DMA,
        ],
        compiler_params=pltpu.CompilerParams(vmem_limit_bytes=24 * 1024 * 1024),
        name="attend",
    )(reach, grouped, bias, own, *earlier)


def per_device(query_proj, key_proj, value_projection, lengths):
    size = lax.axis_size("ctx")
    tokens, kv_heads, head_size = key_proj.shape
    own = jnp.stack((key_proj, value_projection)).transpose(0, 2, 1, 3)
    own = own.reshape(2 * kv_heads, tokens, head_size)
    firsts, seconds = range(0, size, 2), range(1, size, 2)

    def move(array, starts, by):
        return lax.ppermute(array, "ctx", [(i, i + by) for i in starts if 0 <= i + by < size])

    second_mid = move(own, seconds, 2)
    first_mid = move(own, firsts, 2)
    second_near = move(own, firsts, 1)
    prepared = prepare(lengths, query_proj, kv_heads)
    first_far = move(second_mid, seconds[1:], 1)
    first_near = move(second_mid, seconds[1:], -1)
    second_far = move(first_mid, firsts[1:], 1)
    earlier = (second_far, first_near, first_far, second_near, second_mid, first_mid)
    return attend(prepared, own, earlier)


def solution(mesh):
    return jax.shard_map(
        per_device,
        mesh=mesh,
        in_specs=(
            P(("dp", "ctx"), None, None),
            P(("dp", "ctx"), None, None),
            P(("dp", "ctx"), None, None),
            P("dp"),
        ),
        out_specs=(P(("dp", "ctx"), None, None), P(None, ("dp", "ctx"))),
        check_vma=False,
    )
```
